256 devices in a mesh: stretch: 4 (over z_lo, core), seq: 64 (over x, y, z_hi).
Axes of the slice: x: 4, y: 4, z: 8 (z_hi: 4, z_lo: 2; z = z_hi * 2 + z_lo), core: 2. Of those that a mesh axis runs over, the one named last changes fastest.
Arguments:
- queries: bfloat16 [4, 3072, 4096], P('stretch', 'seq'), may hold values from -30 to 30
- keys: bfloat16 [4, 3072, 4096], P('stretch', 'seq'), may hold values from -30 to 30
- values: bfloat16 [4, 3072, 4096], P('stretch', 'seq'), may hold values from -6 to 6
- levels: int32 [4], replicated, may hold values from 0 to 63
- gate_table: float32 [64, 4096], replicated, may hold values from 0.25 to 2
Outputs:
- blended: bfloat16 [4, 3072, 4096], P('stretch', 'seq')
The draws below stay inside these ranges and needn't reach their ends.
All inputs are finite; a program needn't handle non-finite values.
Results may differ from the reference program's by a relative error of at most 0.0095.
Values may be sent and summed in bfloat16 or wider, within the bound.
No kernel may reach another device: no remote copies, remote signals or barrier semaphores. Data moves between devices by JAX's collectives and lax.ppermute only.
A program may use at most 64 MiB of HBM per device.

```python
import math
import jax
import jax.numpy as jnp
from jax import lax

H = 32
DH = 128
LEVELS = 64
STRETCHES = 4
STRETCH_TOK = 3072


def key_field(key):
    sample = jax.random.normal(jax.random.fold_in(key, 101), (STRETCHES, STRETCH_TOK, H * DH), jnp.float32)
    return jnp.clip(sample, -6.0, 6.0)


def draw_keys(key, part):
    base_field = key_field(key)
    return jnp.clip(base_field, -30.0, 30.0).astype(jnp.bfloat16)


def draw_queries(key, part):
    key = jax.random.fold_in(key, 5)
    fresh = jnp.clip(jax.random.normal(key, (STRETCHES, STRETCH_TOK, H * DH), jnp.float32), -6.0, 6.0)
    return jnp.clip(fresh, -30.0, 30.0).astype(jnp.bfloat16)


def touch_ends(array, stream_key, low, top_value):
    longest = array.shape.index(max(array.shape))
    spots = []
    for shift in (0, 1):
        where = [jax.random.randint(jax.random.fold_in(stream_key, axis), (), 0, length) for axis, length in enumerate(array.shape)]
        where[longest] = (where[longest] + shift) % array.shape[longest]
        spots.append(tuple(where))
    return array.at[spots[0]].set(low).at[spots[1]].set(top_value)


def level_of(stream_key, dims, pieces, least, largest):
    level, own = 1.0, jax.random.fold_in(stream_key, 6)
    for dim, blocks in pieces:
        steps = jnp.exp(jax.random.uniform(jax.random.fold_in(own, dim), (blocks,), jnp.float32, least / len(pieces), largest / len(pieces)))
        level = level * jnp.repeat(steps, dims[dim] // blocks).reshape([-1 if axis == dim else 1 for axis in range(len(dims))])
    return level


def gaussian(key, dims, deviation, bound, shards=(), held_as=jnp.bfloat16):
    loudness = level_of(key, dims, shards, -0.22, 0.18) if shards else 1.0
    drawn = jax.random.normal(key, dims, jnp.float32) * deviation * loudness
    return jnp.minimum(jnp.maximum(drawn, -bound), bound).astype(held_as)


def setup_inputs(seed: int = 0) -> dict:
    seeds = jax.random.split(jax.random.key(seed), 6)
    queries = draw_queries(jax.random.fold_in(seeds[5], 71), 0)
    keys = draw_keys(jax.random.fold_in(seeds[5], 71), 0)
    values = gaussian(seeds[2], (STRETCHES, STRETCH_TOK, H * DH), 1.0, 6.0, ((0, 4), (1, 64)))
    levels = touch_ends(jax.random.randint(seeds[3], (STRETCHES,), 0, LEVELS), jax.random.fold_in(seeds[3], 1), 0, LEVELS - 1).astype(jnp.int32)
    gate_table = jnp.clip(jax.random.uniform(seeds[4], (LEVELS, H * DH), jnp.float32, 0.25, 2.0), 0.25, 2.0)
    return dict(queries=queries, keys=keys, values=values, levels=levels, gate_table=gate_table)


def one_head(triple):
    head_query, head_keys, head_values = triple
    score_scale = 1.0 / math.sqrt(DH)
    scores = jnp.dot(head_query, head_keys.T, preferred_element_type=jnp.float32) * score_scale
    peak_value = lax.optimization_barrier(jnp.max(scores, axis=1, keepdims=True))
    weights = jnp.exp(scores - peak_value)
    denominator = lax.optimization_barrier(jnp.sum(weights, axis=1, keepdims=True))
    mixture = jnp.dot(weights.astype(jnp.bfloat16), head_values, preferred_element_type=jnp.float32)
    return (mixture / denominator).astype(jnp.bfloat16)

def reference(queries, keys, values, levels, gate_table):
    results = []
    for stretch_index in range(STRETCHES):
        seen = (stretch_index + 1) * STRETCH_TOK
        head_query = queries[stretch_index].reshape(STRETCH_TOK, H, DH).transpose(1, 0, 2)
        head_keys = keys[:stretch_index + 1].reshape(seen, H, DH).transpose(1, 0, 2)
        head_values = values[:stretch_index + 1].reshape(seen, H, DH).transpose(1, 0, 2)
        attended = lax.map(one_head, (head_query, head_keys, head_values))
        attended = attended.transpose(1, 0, 2).reshape(STRETCH_TOK, H * DH)
        gate_row = gate_table[levels[stretch_index]]
        results.append((gate_row[None, :] * attended.astype(jnp.float32)).astype(jnp.bfloat16))
    return jnp.stack(results)
```

```python
from functools import partial
import math

import jax
import jax.numpy as jnp
from jax import lax
from jax.experimental import pallas as pl
from jax.experimental.pallas import tpu as pltpu
from jax.sharding import PartitionSpec as P

H = 32
DH = 128
AXES = ("stretch", "seq")
SCALE = math.log2(math.e) / math.sqrt(DH)
ROWS = 512
KEYS = 512
VMEM = 56 * 2**20


def exchange(flip_stretch, flip_seq, keep=lambda stretch: True):
    return [
        (c * 64 + s, (c ^ flip_stretch) * 64 + (s ^ flip_seq))
        for c in range(4)
        for s in range(64)
        if keep(c)
    ]


def send(array, pairs):
    return lax.ppermute(array, AXES, pairs)


def softmax_blocks(q, blocks):
    peak = total = mixture = None
    for load_key, load_value in blocks:
        scores = (
            lax.dot_general(
                q, load_key(), (((1,), (1,)), ((), ())), preferred_element_type=jnp.float32
            )
            * SCALE
        )
        block_peak = jnp.max(scores, axis=1, keepdims=True)
        new_peak = block_peak if peak is None else jnp.maximum(peak, block_peak)
        weights = jnp.exp2(scores - new_peak)
        value = load_value()
        value = jnp.concatenate([value, jnp.ones_like(value)], axis=1)
        part = jnp.dot(weights.astype(jnp.bfloat16), value, preferred_element_type=jnp.float32)
        if peak is not None:
            part = mixture * jnp.exp2(peak - new_peak) + part
        mixture, peak = part, new_peak
    total = mixture[:, DH:]
    return mixture[:, :DH] / total, peak + jnp.log2(total)


def loaders(pick, span):
    return [
        (partial(pick, 0, slice(at, at + KEYS)), partial(pick, 1, slice(at, at + KEYS)))
        for at in range(0, span, KEYS)
    ]


def store(mixture_ref, level_ref, mixture, level):
    mixture_ref[...] = mixture.astype(mixture_ref.dtype)
    level_ref[...] = level.T[:8]


def own_kernel(q_ref, near_ref, far_ref, mixture_ref, level_ref):
    blocks = []
    for ref in (near_ref, far_ref):
        blocks += loaders(lambda which, at, ref=ref: ref[which, at, :], ref.shape[1])
    store(mixture_ref, level_ref, *softmax_blocks(q_ref[...], blocks))


def pair_kernel(
    where_ref, q_ref, q_core_ref, x_ref, core_ref, mixture_ref, level_ref
):
    first = where_ref[1] == 0
    q = jnp.where(first, q_core_ref[...], q_ref[...])

    def pick(which, at):
        return jnp.where(first, x_ref[which, at, :], core_ref[which, at, :])

    store(mixture_ref, level_ref, *softmax_blocks(q, loaders(pick, x_ref.shape[1])))


def chip_kernel(
    where_ref, q_ref, z_ref, zv_ref, zc_ref, x_ref, xc_ref, mixture_ref, level_ref
):
    even = where_ref[0] == 0
    here = pl.ds(pl.program_id(0) * ROWS, ROWS)
    q = jnp.where(even, z_ref[here, :], q_ref[...])

    def pick(which, at):
        z = (z_ref, zv_ref)[which][at, :]
        return jnp.where(even, x_ref[which, at, :], z)

    def pick_core(which, at):
        return jnp.where(even, xc_ref[which, at, :], zc_ref[which, at, :])

    span = x_ref.shape[1]
    store(
        mixture_ref,
        level_ref,
        *softmax_blocks(q, loaders(pick, span) + loaders(pick_core, span)),
    )


def merge_kernel(where_ref, gate_ref, own, own_l, pair, pair_l, pair_in, pair_in_l, chip, chip_l, chip_in, chip_in_l, out_ref):
    odd = where_ref[0] == 1
    second = where_ref[1] == 1
    parts = [(own, own_l, None)]
    parts += [(pair, pair_l, second), (pair_in, pair_in_l, second)]
    parts += [(chip, chip_l, odd), (chip_in, chip_in_l, odd)]
    levels = []
    for _, level_ref, use in parts:
        level = jnp.broadcast_to(level_ref[0:1, :], (DH, level_ref.shape[1]))
        if use is not None:
            level = jnp.where(use, level, -jnp.inf)
        levels.append(level)
    top = levels[0]
    for level in levels[1:]:
        top = jnp.maximum(top, level)
    weights = [jnp.exp2(level - top) for level in levels]
    total = sum(weights[1:], weights[0])
    mixture = 0.0
    for (ref, _, use), weight in zip(parts, weights):
        part = ref[...].astype(jnp.float32) * (weight / total).T
        if use is not None:
            part = jnp.where(use, part, 0.0)
        mixture += part
    attended = mixture.astype(jnp.bfloat16).astype(jnp.float32)
    out_ref[...] = (gate_ref[...] * attended).astype(jnp.bfloat16)


def run(kernel, name, scalars, rows_in, whole_in, span, keys_seen):
    def rows(ndim):
        return pl.BlockSpec((ROWS, DH), lambda i, *_: (i, 0))

    in_specs = [rows(a.ndim) for a in rows_in]
    in_specs += [
        pl.BlockSpec(a.shape, lambda i, *_, n=a.ndim: (0,) * n) for a in whole_in
    ]
    return pl.pallas_call(
        kernel,
        grid_spec=pltpu.PrefetchScalarGridSpec(
            num_scalar_prefetch=len(scalars),
            grid=(span // ROWS,),
            in_specs=in_specs,
            out_specs=[rows(2), pl.BlockSpec((8, ROWS), lambda i, *_: (0, i))],
        ),
        out_shape=[
            jax.ShapeDtypeStruct((span, DH), jnp.bfloat16),
            jax.ShapeDtypeStruct((8, span), jnp.float32),
        ],
        compiler_params=pltpu.CompilerParams(vmem_limit_bytes=VMEM),
        cost_estimate=pl.CostEstimate(
            flops=8 * span * keys_seen * DH, bytes_accessed=0, transcendentals=span * keys_seen
        ),
        name=name,
    )(*scalars, *rows_in, *whole_in)


def merge(where, gate, parts, span):
    specs = []
    for _ in range(len(parts) // 2):
        specs.append(pl.BlockSpec((ROWS, DH), lambda i, *_: (i, 0)))
        specs.append(pl.BlockSpec((8, ROWS), lambda i, *_: (0, i)))
    return pl.pallas_call(
        merge_kernel,
        grid_spec=pltpu.PrefetchScalarGridSpec(
            num_scalar_prefetch=1,
            grid=(span // ROWS,),
            in_specs=[pl.BlockSpec((1, DH), lambda i, *_: (0, 0))] + specs,
            out_specs=pl.BlockSpec((ROWS, DH), lambda i, *_: (i, 0)),
        ),
        out_shape=jax.ShapeDtypeStruct((span, DH), jnp.bfloat16),
        compiler_params=pltpu.CompilerParams(vmem_limit_bytes=VMEM),
        name="merge",
    )(where, gate, *parts)


def local(queries, keys, values, levels, gate_table):
    tokens = queries.shape[1]
    half = tokens // 2
    span = 64 * half
    stretch = lax.axis_index("stretch")
    seq = lax.axis_index("seq")
    where = jnp.stack([stretch // 2, stretch % 2]).astype(jnp.int32)
    head = 16 * (seq // 32) + seq % 16
    gate = lax.dynamic_slice(gate_table, (levels[stretch], head * DH), (1, DH))

    qkv = jnp.concatenate([queries, keys, values])
    qkv = qkv.reshape(3, 2, half, 2, 16, DH).transpose(3, 1, 4, 0, 2, 5)
    qkv = lax.all_to_all(qkv.reshape(64, 3, half, DH), "seq", 0, 0, tiled=True)
    qkv = qkv.transpose(1, 0, 2, 3).reshape(3, span, DH)
    q, kv = qkv[0], qkv[1:]

    core = exchange(1, 0)
    kv_x = send(kv, exchange(0, 16))
    z = send(jnp.where(where[0] == 0, kv[0], q), exchange(2, 0))
    zv = send(kv[1], exchange(2, 0, lambda stretch: stretch < 2))
    kv_c = send(kv, core)
    q_c = send(q, core)
    kv_xc = send(kv_x, core)
    zc = send(jnp.stack([z, zv]), core)

    chip = run(chip_kernel, "chip", [where], [q], [z, zv, zc, kv_x, kv_xc], span, 2 * span)
    chip_in = [send(a, exchange(2, 0, lambda stretch: stretch < 2)) for a in chip]
    pair = run(pair_kernel, "pair", [where], [q, q_c], [kv_x, kv_c], span, span)
    pair_in = [send(a, exchange(1, 0, lambda stretch: stretch % 2 == 0)) for a in pair]
    own = run(own_kernel, "own", [], [q], [kv, kv_x], span, 2 * span)
    mixture = merge(where, gate, [*own, *pair, *pair_in, *chip, *chip_in], span)

    result = lax.all_to_all(mixture.reshape(64, half, DH), "seq", 0, 0, tiled=True)
    result = result.reshape(2, 2, 16, half, DH).transpose(1, 3, 0, 2, 4)
    return result.reshape(1, tokens, H * DH)


def solution(mesh):
    placed = (
        P("stretch", "seq", None),
        P("stretch", "seq", None),
        P("stretch", "seq", None),
        P(),
        P(),
    )
    return jax.shard_map(
        local, mesh=mesh, in_specs=placed, out_specs=P("stretch", "seq", None), check_vma=False
    )
```

```python
from functools import partial
import math

import jax
import jax.numpy as jnp
from jax import lax
from jax.experimental import pallas as pl
from jax.experimental.pallas import tpu as pltpu
from jax.sharding import PartitionSpec as P

H = 32
DH = 128
AXES = ("stretch", "seq")
SCALE = math.log2(math.e) / math.sqrt(DH)
ROWS = 512
KEYS = 512
VMEM = 24 * 2**20
F32 = jnp.float32
BF16 = jnp.bfloat16


def exchange(flip_stretch, flip_seq, keep=lambda stretch: True):
    return [
        (c * 64 + s, (c ^ flip_stretch) * 64 + (s ^ flip_seq))
        for c in range(4)
        for s in range(64)
        if keep(c)
    ]


def send(array, pairs):
    return lax.ppermute(array, AXES, pairs)


def score(q, key):
    return (
        lax.dot_general(q, key, (((1,), (1,)), ((), ())), preferred_element_type=F32) * SCALE
    )


def attend(q_ref, blocks, finish):
    work = [
        (key_ref, value_ref, at)
        for key_ref, value_ref in blocks
        for at in range(0, key_ref.shape[0], KEYS)
    ]

    def step(index, carry):
        rows = pl.ds(pl.multiple_of(index * ROWS, ROWS), ROWS)
        q = q_ref[rows, :]

        def scores_of(number):
            key_ref, _, at = work[number]
            return score(q, key_ref[at : at + KEYS, :])

        coming = scores_of(0)
        mixture = peak = None
        for number, (_, value_ref, at) in enumerate(work):
            scores = coming
            if number + 1 < len(work):
                coming = scores_of(number + 1)
            block_peak = jnp.max(scores, axis=1, keepdims=True)
            new_peak = block_peak if peak is None else jnp.maximum(peak, block_peak)
            weights = jnp.exp2(scores - new_peak).astype(BF16)
            value = value_ref[at : at + KEYS, :]
            value = jnp.concatenate([value, jnp.ones_like(value)], axis=1)
            part = jnp.dot(weights, value, preferred_element_type=F32)
            if peak is not None:
                part = mixture * jnp.exp2(peak - new_peak) + part
            mixture, peak = part, new_peak
        wide = jnp.broadcast_to(peak, (ROWS, DH))
        finish(index, rows, mixture[:, :DH], mixture[:, DH:], wide)
        return carry

    lax.fori_loop(0, q_ref.shape[0] // ROWS, step, None)


def pair(ref):
    return ref.at[0], ref.at[1]


def join(first, second):
    peak = jnp.maximum(first[2], second[2])
    left, right = jnp.exp2(first[2] - peak), jnp.exp2(second[2] - peak)
    return (
        first[0] * left + second[0] * right,
        first[1] * left + second[1] * right,
        peak,
    )


def near_kernel(q_ref, kv_ref, kvc_ref, out_ref):
    def first(index, rows, *result):
        for i in range(3):
            out_ref[i, rows, :] = result[i]

    def then(index, rows, *result):
        first(index, rows, *join(result, [out_ref[i, rows, :] for i in range(3)]))

    attend(q_ref, [pair(kv_ref)], first)

    @pl.when(lax.axis_index("stretch") % 2 == 1)
    def _():
        attend(q_ref, [pair(kvc_ref)], then)


def far_kernel(q_ref, kv_ref, kvc_ref, near_ref, chip_ref, out_ref, level_ref, state, chip_level):
    stretch = lax.axis_index("stretch")
    second = stretch % 2 == 1
    odd = stretch >= 2
    unpack_level(chip_ref, chip_level)

    def first(index, rows, *result):
        result = join(result, [near_ref[i, rows, :] for i in range(3)])
        mixture = chip_ref[rows, :].astype(F32)
        level = jnp.where(odd, chip_level[level_rows(index), :], -jnp.inf)
        level = jnp.broadcast_to(columns(level)[0], (ROWS, DH))
        result = join(result, (mixture, 1.0, level))
        for i in range(3):
            state[i, rows, :] = result[i]

    def then(index, rows, *result):
        result = join(result, [state[i, rows, :] for i in range(3)])
        for i in range(3):
            state[i, rows, :] = result[i]

    attend(q_ref, [pair(kv_ref)], first)

    @pl.when(second)
    def _():
        attend(q_ref, [pair(kvc_ref)], then)

    for index in range(q_ref.shape[0] // ROWS):
        rows = slice(index * ROWS, index * ROWS + ROWS)
        out_ref[rows, :] = state[0, rows, :] / state[1, rows, :]
        level_ref[level_rows(index), :] = level_of(state[2, rows, :], state[1, rows, :])


def level_rows(index):
    return pl.ds(index * 8 if isinstance(index, int) else pl.multiple_of(index * 8, 8), 8)


def level_of(peak, total):
    level = (peak + jnp.log2(total)).T[:1, :]
    groups = [level[:, at : at + DH] for at in range(0, ROWS, DH)]
    return jnp.concatenate((groups * 8)[:8], axis=0)


def columns(*groups):
    lines = [
        jnp.concatenate([group[at : at + 1, :] for at in range(ROWS // DH)], axis=1)
        for group in groups
    ]
    lines += [lines[0]] * (8 - len(lines))
    table = jnp.concatenate(lines, axis=0).T
    return [table[:, at : at + 1] for at in range(len(groups))]


def message_rows(span):
    return span + 3 * level_count(span)


def level_count(span):
    return -(-span // ROWS * 8 // 16) * 16


def pack_level(ref, levels):
    count = levels.shape[0]
    rest = levels[...]
    for part in range(3):
        piece = rest.astype(BF16)
        rest = rest - piece.astype(F32)
        start = ref.shape[0] - (3 - part) * count
        ref[start : start + count, :] = piece


def unpack_level(ref, levels):
    count = levels.shape[0]
    parts = [
        ref[ref.shape[0] - (3 - part) * count : ref.shape[0] - (2 - part) * count, :].astype(F32)
        for part in range(3)
    ]
    levels[...] = parts[0] + parts[1] + parts[2]


def chip_kernel(q_ref, z_ref, zc_ref, x_ref, xc_ref, out_ref, levels):
    even = lax.axis_index("stretch") < 2
    levels[...] = jnp.zeros_like(levels)

    def finish(index, rows, mixture, total, peak):
        out_ref[rows, :] = (mixture / total).astype(BF16)
        levels[level_rows(index), :] = level_of(peak, total)

    @pl.when(even)
    def _():
        attend(z_ref.at[0], [pair(x_ref), pair(xc_ref)], finish)

    @pl.when(jnp.logical_not(even))
    def _():
        attend(q_ref, [pair(z_ref), pair(zc_ref)], finish)

    pack_level(out_ref, levels)


def merge_kernel(levels_ref, gate_ref, own_ref, level_ref, chip_ref, out_ref, chip_levels):
    stretch = lax.axis_index("stretch")
    seq = lax.axis_index("seq")
    odd = stretch >= 2
    head = 16 * (seq // 32) + seq % 16
    lanes = pl.ds(pl.multiple_of(head * DH, DH), DH)
    noise = levels_ref[stretch]
    tile = gate_ref[pl.ds(pl.multiple_of(noise // 8 * 8, 8), 8), lanes]
    mine = lax.broadcasted_iota(jnp.int32, tile.shape, 0) == noise % 8
    gate = jnp.sum(jnp.where(mine, tile, 0.0), axis=0, keepdims=True)
    unpack_level(chip_ref, chip_levels)
    for index in range(own_ref.shape[0] // ROWS):
        rows = slice(index * ROWS, index * ROWS + ROWS)
        level = level_ref[level_rows(index), :]
        chip_level = jnp.where(odd, chip_levels[level_rows(index), :], -jnp.inf)
        top = jnp.maximum(level, chip_level)
        left, right = jnp.exp2(level - top), jnp.exp2(chip_level - top)
        left, right = columns(left / (left + right), right / (left + right))
        other = jnp.where(odd, chip_ref[rows, :].astype(F32), 0.0)
        attended = (own_ref[rows, :] * left + other * right).astype(BF16).astype(F32)
        out_ref[rows, :] = (gate * attended).astype(BF16)


HELD = pl.BlockSpec(memory_space=pltpu.VMEM)


def call(kernel, name, ins, in_specs, out_shape, out_spec, scratch, units):
    return pl.pallas_call(
        kernel,
        in_specs=in_specs,
        out_specs=out_spec,
        out_shape=out_shape,
        scratch_shapes=scratch,
        compiler_params=pltpu.CompilerParams(vmem_limit_bytes=VMEM),
        cost_estimate=pl.CostEstimate(
            flops=units * 8 * 1536 * 1536 * DH,
            bytes_accessed=2**20,
            transcendentals=units * 1536 * 1536,
        ),
        name=name,
    )(*ins)


def local(queries, keys, values, levels, gate_table):
    tokens = queries.shape[1]
    half = tokens // 2
    span = 64 * half
    even_chip = lax.axis_index("stretch") < 2
    qkv = jnp.concatenate([queries, keys, values])
    qkv = qkv.reshape(3, 2, half, 2, 16, DH).transpose(3, 1, 4, 0, 2, 5).reshape(64, 3, half, DH)
    qkv = lax.all_to_all(qkv, "seq", 0, 0, tiled=True)
    qkv = qkv.transpose(1, 0, 2, 3).reshape(3, span, DH)
    q, kv = qkv[0], qkv[1:]

    core, x, z = exchange(1, 0), exchange(0, 16), exchange(2, 0)
    odd_core = exchange(1, 0, lambda stretch: stretch >= 2)
    kv_x = send(kv, x)
    z = send(jnp.stack([jnp.where(even_chip, kv[0], q), kv[1]]), z)
    kv_core = send(kv, core)

    state = jax.ShapeDtypeStruct((3, span, DH), F32)
    message = jax.ShapeDtypeStruct((message_rows(span), DH), BF16)
    level_shape = (level_count(span), DH)
    level_scratch = pltpu.VMEM(level_shape, F32)
    own = [jax.ShapeDtypeStruct((span, DH), F32), jax.ShapeDtypeStruct(level_shape, F32)]
    near = call(near_kernel, "near", [q, kv, kv_core], [HELD] * 3, state, HELD, [], 2)
    kv_x, z, near = lax.optimization_barrier((kv_x, z, near))
    kv_x_core = send(kv_x, core)
    z_core = send(z, odd_core)
    chip = call(
        chip_kernel, "chip", [q, z, z_core, kv_x, kv_x_core], [HELD] * 5, message, HELD,
        [level_scratch], 2,
    )
    chip_in = send(chip, exchange(2, 0, lambda stretch: stretch < 2))
    far = call(
        far_kernel, "far", [q, kv_x, kv_x_core, near, chip], [HELD] * 5, own, [HELD] * 2,
        [pltpu.VMEM(state.shape, F32), level_scratch], 2,
    )
    mixture = call(
        merge_kernel, "merge", [levels, gate_table, *far, chip_in],
        [pl.BlockSpec(memory_space=pltpu.SMEM)] + [HELD] * 4,
        jax.ShapeDtypeStruct((span, DH), BF16), HELD, [level_scratch], 0,
    )
    result = lax.all_to_all(mixture.reshape(64, half, DH), "seq", 0, 0, tiled=True)
    result = result.reshape(2, 2, 16, half, DH).transpose(1, 3, 0, 2, 4)
    return result.reshape(1, tokens, H * DH)


def solution(mesh):
    placed = (
        P("stretch", "seq", None),
        P("stretch", "seq", None),
        P("stretch", "seq", None),
        P(),
        P(),
    )
    return jax.shard_map(
        local, mesh=mesh, in_specs=placed, out_specs=P("stretch", "seq", None), check_vma=False
    )
```

```python
from functools import partial
import math

import jax
import jax.numpy as jnp
from jax import lax
from jax.experimental import pallas as pl
from jax.experimental.pallas import tpu as pltpu
from jax.sharding import PartitionSpec as P

H = 32
DH = 128
AXES = ("stretch", "seq")
SCALE = math.log2(math.e) / math.sqrt(DH)
ROWS = 512
KEYS = 512
VMEM = 24 * 2**20
F32 = jnp.float32
BF16 = jnp.bfloat16


def exchange(flip_stretch, flip_seq, keep=lambda stretch: True):
    return [
        (c * 64 + s, (c ^ flip_stretch) * 64 + (s ^ flip_seq))
        for c in range(4)
        for s in range(64)
        if keep(c)
    ]


def send(array, pairs):
    return lax.ppermute(array, AXES, pairs)


def score(q, key):
    return (
        lax.dot_general(q, key, (((1,), (1,)), ((), ())), preferred_element_type=F32) * SCALE
    )


def attend(q_ref, blocks, finish):
    work = [
        (key_ref, value_ref, at)
        for key_ref, value_ref in blocks
        for at in range(0, key_ref.shape[0], KEYS)
    ]

    def step(index, carry):
        rows = pl.ds(pl.multiple_of(index * ROWS, ROWS), ROWS)
        q = q_ref[rows, :]

        def scores_of(number):
            key_ref, _, at = work[number]
            return score(q, key_ref[at : at + KEYS, :])

        coming = scores_of(0)
        mixture = peak = None
        for number, (_, value_ref, at) in enumerate(work):
            scores = coming
            if number + 1 < len(work):
                coming = scores_of(number + 1)
            block_peak = jnp.max(scores, axis=1, keepdims=True)
            new_peak = block_peak if peak is None else jnp.maximum(peak, block_peak)
            weights = jnp.exp2(scores - new_peak).astype(BF16)
            value = value_ref[at : at + KEYS, :]
            value = jnp.concatenate([value, jnp.ones_like(value)], axis=1)
            part = jnp.dot(weights, value, preferred_element_type=F32)
            if peak is not None:
                part = mixture * jnp.exp2(peak - new_peak) + part
            mixture, peak = part, new_peak
        wide = jnp.broadcast_to(peak, (ROWS, DH))
        finish(index, rows, mixture[:, :DH], mixture[:, DH:], wide)
        return carry

    lax.fori_loop(0, q_ref.shape[0] // ROWS, step, None)


def pair(ref):
    return ref.at[0], ref.at[1]


def join(first, second):
    peak = jnp.maximum(first[2], second[2])
    left, right = jnp.exp2(first[2] - peak), jnp.exp2(second[2] - peak)
    return (
        first[0] * left + second[0] * right,
        first[1] * left + second[1] * right,
        peak,
    )


def near_kernel(q_ref, kv_ref, kvc_ref, out_ref):
    def first(index, rows, *result):
        for i in range(3):
            out_ref[i, rows, :] = result[i]

    def then(index, rows, *result):
        first(index, rows, *join(result, [out_ref[i, rows, :] for i in range(3)]))

    attend(q_ref, [pair(kv_ref)], first)

    @pl.when(lax.axis_index("stretch") % 2 == 1)
    def _():
        attend(q_ref, [pair(kvc_ref)], then)


def far_kernel(q_ref, kv_ref, kvc_ref, near_ref, out_ref, level_ref, state):
    second = lax.axis_index("stretch") % 2 == 1

    def first(index, rows, *result):
        result = join(result, [near_ref[i, rows, :] for i in range(3)])
        for i in range(3):
            state[i, rows, :] = result[i]

    def then(index, rows, *result):
        result = join(result, [state[i, rows, :] for i in range(3)])
        for i in range(3):
            state[i, rows, :] = result[i]

    attend(q_ref, [pair(kv_ref)], first)

    @pl.when(second)
    def _():
        attend(q_ref, [pair(kvc_ref)], then)

    for index in range(q_ref.shape[0] // ROWS):
        rows = slice(index * ROWS, index * ROWS + ROWS)
        out_ref[rows, :] = state[0, rows, :] / state[1, rows, :]
        level_ref[level_rows(index), :] = level_of(state[2, rows, :], state[1, rows, :])


def level_rows(index):
    return pl.ds(index * 8 if isinstance(index, int) else pl.multiple_of(index * 8, 8), 8)


def level_of(peak, total):
    level = (peak + jnp.log2(total)).T[:1, :]
    groups = [level[:, at : at + DH] for at in range(0, ROWS, DH)]
    return jnp.concatenate((groups * 8)[:8], axis=0)


def columns(*groups):
    lines = [
        jnp.concatenate([group[at : at + 1, :] for at in range(ROWS // DH)], axis=1)
        for group in groups
    ]
    lines += [lines[0]] * (8 - len(lines))
    table = jnp.concatenate(lines, axis=0).T
    return [table[:, at : at + 1] for at in range(len(groups))]


def message_rows(span):
    return span + 3 * level_count(span)


def level_count(span):
    return -(-span // ROWS * 8 // 16) * 16


def pack_level(ref, levels):
    count = levels.shape[0]
    rest = levels[...]
    for part in range(3):
        piece = rest.astype(BF16)
        rest = rest - piece.astype(F32)
        start = ref.shape[0] - (3 - part) * count
        ref[start : start + count, :] = piece


def unpack_level(ref, levels):
    count = levels.shape[0]
    parts = [
        ref[ref.shape[0] - (3 - part) * count : ref.shape[0] - (2 - part) * count, :].astype(F32)
        for part in range(3)
    ]
    levels[...] = parts[0] + parts[1] + parts[2]


def chip_near_kernel(q_ref, kv_ref, kvc_ref, out_ref):
    def finish(index, rows, *result):
        for i in range(3):
            out_ref[i, rows, :] = result[i]

    @pl.when(lax.axis_index("stretch") < 2)
    def _():
        attend(q_ref, [pair(kv_ref), pair(kvc_ref)], finish)


def chip_far_kernel(q_ref, kv_ref, kvc_ref, near_ref, out_ref, levels):
    def finish(index, rows, *result):
        mixture, total, peak = join(result, [near_ref[i, rows, :] for i in range(3)])
        out_ref[rows, :] = (mixture / total).astype(BF16)
        levels[level_rows(index), :] = level_of(peak, total)

    @pl.when(lax.axis_index("stretch") < 2)
    def _():
        levels[...] = jnp.zeros_like(levels)
        attend(q_ref, [pair(kv_ref), pair(kvc_ref)], finish)
        pack_level(out_ref, levels)


def merge_kernel(levels_ref, gate_ref, own_ref, level_ref, chip_ref, out_ref, chip_levels):
    stretch = lax.axis_index("stretch")
    seq = lax.axis_index("seq")
    odd = stretch >= 2
    head = 16 * (seq // 32) + seq % 16
    lanes = pl.ds(pl.multiple_of(head * DH, DH), DH)
    noise = levels_ref[stretch]
    tile = gate_ref[pl.ds(pl.multiple_of(noise // 8 * 8, 8), 8), lanes]
    mine = lax.broadcasted_iota(jnp.int32, tile.shape, 0) == noise % 8
    gate = jnp.sum(jnp.where(mine, tile, 0.0), axis=0, keepdims=True)
    unpack_level(chip_ref, chip_levels)
    for index in range(own_ref.shape[0] // ROWS):
        rows = slice(index * ROWS, index * ROWS + ROWS)
        level = level_ref[level_rows(index), :]
        chip_level = jnp.where(odd, chip_levels[level_rows(index), :], -jnp.inf)
        top = jnp.maximum(level, chip_level)
        left, right = jnp.exp2(level - top), jnp.exp2(chip_level - top)
        left, right = columns(left / (left + right), right / (left + right))
        other = jnp.where(odd, chip_ref[rows, :].astype(F32), 0.0)
        attended = (own_ref[rows, :] * left + other * right).astype(BF16).astype(F32)
        out_ref[rows, :] = (gate * attended).astype(BF16)


HELD = pl.BlockSpec(memory_space=pltpu.VMEM)


def call(kernel, name, ins, in_specs, out_shape, out_spec, scratch, units):
    return pl.pallas_call(
        kernel,
        in_specs=in_specs,
        out_specs=out_spec,
        out_shape=out_shape,
        scratch_shapes=scratch,
        compiler_params=pltpu.CompilerParams(vmem_limit_bytes=VMEM),
        cost_estimate=pl.CostEstimate(
            flops=units * 8 * 1536 * 1536 * DH,
            bytes_accessed=2**20,
            transcendentals=units * 1536 * 1536,
        ),
        name=name,
    )(*ins)


def local(queries, keys, values, levels, gate_table):
    tokens = queries.shape[1]
    half = tokens // 2
    span = 64 * half
    qkv = jnp.concatenate([queries, keys, values])
    qkv = qkv.reshape(3, 2, half, 2, 16, DH).transpose(3, 1, 4, 0, 2, 5).reshape(64, 3, half, DH)
    qkv = lax.all_to_all(qkv, "seq", 0, 0, tiled=True)
    qkv = qkv.transpose(1, 0, 2, 3).reshape(3, span, DH)
    q, kv = qkv[0], qkv[1:]

    core = exchange(1, 0)
    kv_x = send(kv, exchange(0, 16))
    kv_core = send(kv, core)
    q_z = send(q, exchange(2, 0, lambda stretch: stretch >= 2))
    state = jax.ShapeDtypeStruct((3, span, DH), F32)
    message = jax.ShapeDtypeStruct((message_rows(span), DH), BF16)
    level_shape = (level_count(span), DH)
    level_scratch = pltpu.VMEM(level_shape, F32)
    own = [jax.ShapeDtypeStruct((span, DH), F32), jax.ShapeDtypeStruct(level_shape, F32)]
    near = call(near_kernel, "near", [q, kv, kv_core], [HELD] * 3, state, HELD, [], 2)
    q_z, near = lax.optimization_barrier((q_z, near))
    chip_near = call(
        chip_near_kernel, "chip_near", [q_z, kv, kv_core], [HELD] * 3, state, HELD, [], 2
    )
    kv_x, near, chip_near = lax.optimization_barrier((kv_x, near, chip_near))
    kv_x_core = send(kv_x, core)
    chip = call(
        chip_far_kernel, "chip_far", [q_z, kv_x, kv_x_core, chip_near], [HELD] * 4, message, HELD,
        [level_scratch], 2,
    )
    chip_in = send(chip, exchange(2, 0, lambda stretch: stretch < 2))
    chip, near = lax.optimization_barrier((chip, near))
    far = call(
        far_kernel, "far", [q, kv_x, kv_x_core, near], [HELD] * 4, own, [HELD] * 2,
        [pltpu.VMEM(state.shape, F32)], 2,
    )
    mixture = call(
        merge_kernel, "merge", [levels, gate_table, *far, chip_in],
        [pl.BlockSpec(memory_space=pltpu.SMEM)] + [HELD] * 4,
        jax.ShapeDtypeStruct((span, DH), BF16), HELD, [level_scratch], 0,
    )
    result = lax.all_to_all(mixture.reshape(64, half, DH), "seq", 0, 0, tiled=True)
    result = result.reshape(2, 2, 16, half, DH).transpose(1, 3, 0, 2, 4)
    return result.reshape(1, tokens, H * DH)


def solution(mesh):
    placed = (
        P("stretch", "seq", None),
        P("stretch", "seq", None),
        P("stretch", "seq", None),
        P(),
        P(),
    )
    return jax.shard_map(
        local, mesh=mesh, in_specs=placed, out_specs=P("stretch", "seq", None), check_vma=False
    )
```

```python
from functools import partial
import math

import jax
import jax.numpy as jnp
from jax import lax
from jax.experimental import pallas as pl
from jax.experimental.pallas import tpu as pltpu
from jax.sharding import PartitionSpec as P

H = 32
DH = 128
AXES = ("stretch", "seq")
SCALE = math.log2(math.e) / math.sqrt(DH)
ROWS = 768
KEYS = 512
VMEM = 24 * 2**20
F32 = jnp.float32
BF16 = jnp.bfloat16


def exchange(flip_stretch, flip_seq, keep=lambda stretch: True):
    return [
        (c * 64 + s, (c ^ flip_stretch) * 64 + (s ^ flip_seq))
        for c in range(4)
        for s in range(64)
        if keep(c)
    ]


def send(array, pairs):
    return lax.ppermute(array, AXES, pairs)


def score(q, key):
    return (
        lax.dot_general(q, key, (((1,), (1,)), ((), ())), preferred_element_type=F32) * SCALE
    )


def attend(q_ref, blocks, finish, first=0, count=None):
    work = [
        (key_ref, value_ref, at)
        for key_ref, value_ref in blocks
        for at in range(0, key_ref.shape[0], KEYS)
    ]

    def step(index, carry):
        rows = pl.ds(pl.multiple_of(index * ROWS, ROWS), ROWS)
        q = q_ref[rows, :]

        def scores_of(number):
            key_ref, _, at = work[number]
            return score(q, key_ref[at : at + KEYS, :])

        coming = scores_of(0)
        mixture = peak = None
        for number, (_, value_ref, at) in enumerate(work):
            scores = coming
            if number + 1 < len(work):
                coming = scores_of(number + 1)
            block_peak = jnp.max(scores, axis=1, keepdims=True)
            new_peak = block_peak if peak is None else jnp.maximum(peak, block_peak)
            weights = jnp.exp2(scores - new_peak).astype(BF16)
            value = value_ref[at : at + KEYS, :]
            value = jnp.concatenate([value, jnp.ones_like(value)], axis=1)
            part = jnp.dot(weights, value, preferred_element_type=F32)
            if peak is not None:
                part = mixture * jnp.exp2(peak - new_peak) + part
            mixture, peak = part, new_peak
        wide = jnp.broadcast_to(peak, (ROWS, DH))
        finish(index, rows, mixture[:, :DH], mixture[:, DH:], wide)
        return carry

    count = q_ref.shape[0] // ROWS if count is None else count
    lax.fori_loop(first, first + count, step, None)


def pair(ref):
    return ref.at[0], ref.at[1]


def join(first, second):
    peak = jnp.maximum(first[2], second[2])
    left, right = jnp.exp2(first[2] - peak), jnp.exp2(second[2] - peak)
    return (
        first[0] * left + second[0] * right,
        first[1] * left + second[1] * right,
        peak,
    )


def by_core(q_ref, blocks, core_block, finish):
    second = lax.axis_index("stretch") % 2 == 1
    pl.when(second)(lambda: attend(q_ref, [*blocks, core_block], finish))
    pl.when(jnp.logical_not(second))(lambda: attend(q_ref, blocks, finish))


def near_kernel(q_ref, kv_ref, kvc_ref, out_ref):
    def finish(index, rows, *result):
        for i in range(3):
            out_ref[i, rows, :] = result[i]

    second = lax.axis_index("stretch") % 2 == 1
    pl.when(second)(lambda: attend(q_ref, [pair(kv_ref), pair(kvc_ref)], finish))
    pl.when(jnp.logical_not(second))(lambda: attend(q_ref, [pair(kv_ref)], finish))


def far_kernel(q_ref, kv_ref, before_ref, out_ref):
    def finish(index, rows, *result):
        result = join(result, [before_ref[i, rows, :] for i in range(3)])
        for i in range(3):
            out_ref[i, rows, :] = result[i]

    attend(q_ref, [pair(kv_ref)], finish)


def last_kernel(q_ref, kv_ref, before_ref, out_ref, level_ref):
    def store(index, rows, mixture, total, peak):
        out_ref[rows, :] = mixture / total
        level_ref[level_rows(index), :] = level_of(peak, total)

    def finish(index, rows, *result):
        store(index, rows, *join(result, [before_ref[i, rows, :] for i in range(3)]))

    second = lax.axis_index("stretch") % 2 == 1

    @pl.when(second)
    def _():
        attend(q_ref, [pair(kv_ref)], finish)

    @pl.when(jnp.logical_not(second))
    def _():
        for index in range(q_ref.shape[0] // ROWS):
            rows = slice(index * ROWS, index * ROWS + ROWS)
            store(index, rows, *[before_ref[i, rows, :] for i in range(3)])


def even_chip():
    return lax.axis_index("stretch") < 2


def level_rows(index):
    return pl.ds(index * 8 if isinstance(index, int) else pl.multiple_of(index * 8, 8), 8)


def level_of(peak, total):
    level = (peak + jnp.log2(total)).T[:1, :]
    groups = [level[:, at : at + DH] for at in range(0, ROWS, DH)]
    return jnp.concatenate((groups * 8)[:8], axis=0)


def columns(*groups):
    lines = [
        jnp.concatenate([group[at : at + 1, :] for at in range(ROWS // DH)], axis=1)
        for group in groups
    ]
    lines += [lines[0]] * (8 - len(lines))
    table = jnp.concatenate(lines, axis=0).T
    return [table[:, at : at + 1] for at in range(len(groups))]


def message_rows(span):
    return span + 3 * level_count(span)


def level_count(span):
    return -(-span // ROWS * 8 // 16) * 16


def pack_level(ref, levels):
    count = levels.shape[0]
    rest = levels[...]
    for part in range(3):
        piece = rest.astype(BF16)
        rest = rest - piece.astype(F32)
        start = ref.shape[0] - (3 - part) * count
        ref[start : start + count, :] = piece


def unpack_level(ref, levels):
    count = levels.shape[0]
    parts = [
        ref[ref.shape[0] - (3 - part) * count : ref.shape[0] - (2 - part) * count, :].astype(F32)
        for part in range(3)
    ]
    levels[...] = parts[0] + parts[1] + parts[2]


def chip_near_kernel(q_ref, kv_ref, kvc_ref, out_ref):
    def finish(index, rows, *result):
        for i in range(3):
            out_ref[i, rows, :] = result[i]

    @pl.when(even_chip())
    def _():
        attend(q_ref, [pair(kv_ref), pair(kvc_ref)], finish)


def chip_far_kernel(block, q_ref, kv_ref, kvc_ref, near_ref, out_ref, levels):
    def finish(index, rows, *result):
        mixture, total, peak = join(result, [near_ref[i, rows, :] for i in range(3)])
        out_ref[:ROWS, :] = (mixture / total).astype(BF16)
        levels[level_rows(0), :] = level_of(peak, total)

    @pl.when(even_chip())
    def _():
        levels[...] = jnp.zeros_like(levels)
        attend(q_ref, [pair(kv_ref), pair(kvc_ref)], finish, block, 1)
        pack_level(out_ref, levels)


def merge_kernel(levels_ref, gate_ref, own_ref, level_ref, *refs):
    *chip_refs, out_ref, chip_levels = refs
    stretch = lax.axis_index("stretch")
    seq = lax.axis_index("seq")
    odd = stretch >= 2
    head = 16 * (seq // 32) + seq % 16
    lanes = pl.ds(pl.multiple_of(head * DH, DH), DH)
    noise = levels_ref[stretch]
    tile = gate_ref[pl.ds(pl.multiple_of(noise // 8 * 8, 8), 8), lanes]
    mine = lax.broadcasted_iota(jnp.int32, tile.shape, 0) == noise % 8
    gate = jnp.sum(jnp.where(mine, tile, 0.0), axis=0, keepdims=True)
    for index, chip_ref in enumerate(chip_refs):
        unpack_level(chip_ref, chip_levels)
        rows = slice(index * ROWS, index * ROWS + ROWS)
        level = level_ref[level_rows(index), :]
        chip_level = jnp.where(odd, chip_levels[level_rows(0), :], -jnp.inf)
        top = jnp.maximum(level, chip_level)
        left, right = jnp.exp2(level - top), jnp.exp2(chip_level - top)
        left, right = columns(left / (left + right), right / (left + right))
        other = jnp.where(odd, chip_ref[:ROWS, :].astype(F32), 0.0)
        attended = (own_ref[rows, :] * left + other * right).astype(BF16).astype(F32)
        out_ref[rows, :] = (gate * attended).astype(BF16)


HELD = pl.BlockSpec(memory_space=pltpu.VMEM)


def call(kernel, name, ins, in_specs, out_shape, out_spec, scratch, aliases=()):
    return pl.pallas_call(
        kernel,
        in_specs=in_specs,
        out_specs=out_spec,
        out_shape=out_shape,
        scratch_shapes=scratch,
        input_output_aliases=dict(aliases),
        compiler_params=pltpu.CompilerParams(vmem_limit_bytes=VMEM),
        cost_estimate=pl.CostEstimate(flops=DH, bytes_accessed=DH, transcendentals=0),
        name=name,
    )(*ins)


def local(queries, keys, values, levels, gate_table):
    tokens = queries.shape[1]
    half = tokens // 2
    span = 64 * half
    qkv = jnp.concatenate([queries, keys, values])
    qkv = qkv.reshape(3, 2, half, 2, 16, DH).transpose(3, 1, 4, 0, 2, 5).reshape(64, 3, half, DH)
    qkv = lax.all_to_all(qkv, "seq", 0, 0, tiled=True)
    qkv = qkv.transpose(1, 0, 2, 3).reshape(3, span, DH)
    q, kv = qkv[0], qkv[1:]

    core = exchange(1, 0)
    kv_x = send(kv, exchange(0, 16))
    kv_core = send(kv, core)
    q_z = send(q, exchange(2, 0, lambda stretch: stretch >= 2))
    state = jax.ShapeDtypeStruct((3, span, DH), F32)
    message = jax.ShapeDtypeStruct((message_rows(ROWS), DH), BF16)
    level_scratch = pltpu.VMEM((level_count(ROWS), DH), F32)
    own_shape = [
        jax.ShapeDtypeStruct((span, DH), F32), jax.ShapeDtypeStruct((level_count(span), DH), F32)
    ]
    near = call(near_kernel, "near", [q, kv, kv_core], [HELD] * 3, state, HELD, [])
    q_z, near = lax.optimization_barrier((q_z, near))
    chip_near = call(
        chip_near_kernel, "chip_near", [q_z, kv, kv_core], [HELD] * 3, state, HELD, []
    )
    kv_x, near, chip_near = lax.optimization_barrier((kv_x, near, chip_near))
    kv_x_core = send(kv_x, core)
    far = call(far_kernel, "far", [q, kv_x, near], [HELD] * 3, state, HELD, [], {2: 0})
    kv_x_core, far, chip_near = lax.optimization_barrier((kv_x_core, far, chip_near))

    def lend(block, before):
        chip = call(
            partial(chip_far_kernel, block), f"chip_far{block}", [q_z, kv_x, kv_x_core, before],
            [HELD] * 4, message, HELD, [level_scratch],
        )
        return chip, send(chip, exchange(2, 0, lambda stretch: stretch < 2))

    chip, first_in = lend(0, chip_near)
    chip, chip_near = lax.optimization_barrier((chip, chip_near))
    chip, second_in = lend(1, chip_near)
    first_in, chip, far = lax.optimization_barrier((first_in, chip, far))
    own = call(
        last_kernel, "last", [q, kv_x_core, far], [HELD] * 3, own_shape, [HELD] * 2, []
    )
    mixture = call(
        merge_kernel, "merge", [levels, gate_table, *own, first_in, second_in],
        [pl.BlockSpec(memory_space=pltpu.SMEM)] + [HELD] * 5,
        jax.ShapeDtypeStruct((span, DH), BF16), HELD, [level_scratch],
    )
    result = lax.all_to_all(mixture.reshape(64, half, DH), "seq", 0, 0, tiled=True)
    result = result.reshape(2, 2, 16, half, DH).transpose(1, 3, 0, 2, 4)
    return result.reshape(1, tokens, H * DH)


def solution(mesh):
    placed = (
        P("stretch", "seq", None),
        P("stretch", "seq", None),
        P("stretch", "seq", None),
        P(),
        P(),
    )
    return jax.shard_map(
        local, mesh=mesh, in_specs=placed, out_specs=P("stretch", "seq", None), check_vma=False
    )
```

```python
from functools import partial
import math

import jax
import jax.numpy as jnp
from jax import lax
from jax.experimental import pallas as pl
from jax.experimental.pallas import tpu as pltpu
from jax.sharding import PartitionSpec as P

H = 32
DH = 128
AXES = ("stretch", "seq")
SCALE = math.log2(math.e) / math.sqrt(DH)
ROWS = 768
KEYS = 512
VMEM = 24 * 2**20
F32 = jnp.float32
BF16 = jnp.bfloat16


def exchange(flip_stretch, flip_seq, keep=lambda stretch: True):
    return [
        (c * 64 + s, (c ^ flip_stretch) * 64 + (s ^ flip_seq))
        for c in range(4)
        for s in range(64)
        if keep(c)
    ]


def send(array, pairs):
    return lax.ppermute(array, AXES, pairs)


def score(q, key):
    return (
        lax.dot_general(q, key, (((1,), (1,)), ((), ())), preferred_element_type=F32) * SCALE
    )


def attend(q_ref, blocks, finish, first=0, count=None):
    work = [
        (key_ref, value_ref, at)
        for key_ref, value_ref in blocks
        for at in range(0, key_ref.shape[0], KEYS)
    ]

    def step(index, carry):
        rows = pl.ds(pl.multiple_of(index * ROWS, ROWS), ROWS)
        q = q_ref[rows, :]

        def scores_of(number):
            key_ref, _, at = work[number]
            return score(q, key_ref[at : at + KEYS, :])

        coming = scores_of(0)
        mixture = peak = None
        for number, (_, value_ref, at) in enumerate(work):
            scores = coming
            if number + 1 < len(work):
                coming = scores_of(number + 1)
            block_peak = jnp.max(scores, axis=1, keepdims=True)
            new_peak = block_peak if peak is None else jnp.maximum(peak, block_peak)
            weights = jnp.exp2(scores - new_peak).astype(BF16)
            value = value_ref[at : at + KEYS, :]
            value = jnp.concatenate([value, jnp.ones_like(value)], axis=1)
            part = jnp.dot(weights, value, preferred_element_type=F32)
            if peak is not None:
                part = mixture * jnp.exp2(peak - new_peak) + part
            mixture, peak = part, new_peak
        wide = jnp.broadcast_to(peak, (ROWS, DH))
        finish(index, rows, mixture[:, :DH], mixture[:, DH:], wide)
        return carry

    count = q_ref.shape[0] // ROWS if count is None else count
    lax.fori_loop(first, first + count, step, None)


def pair(ref):
    return ref.at[0], ref.at[1]


def join(first, second):
    peak = jnp.maximum(first[2], second[2])
    left, right = jnp.exp2(first[2] - peak), jnp.exp2(second[2] - peak)
    return (
        first[0] * left + second[0] * right,
        first[1] * left + second[1] * right,
        peak,
    )


def by_core(q_ref, blocks, core_block, finish):
    second = lax.axis_index("stretch") % 2 == 1
    pl.when(second)(lambda: attend(q_ref, [*blocks, core_block], finish))
    pl.when(jnp.logical_not(second))(lambda: attend(q_ref, blocks, finish))


def near_kernel(q_ref, kv_ref, kc_ref, vc_ref, out_ref):
    def finish(index, rows, *result):
        for i in range(3):
            out_ref[i, rows, :] = result[i]

    second = lax.axis_index("stretch") % 2 == 1
    pl.when(second)(lambda: attend(q_ref, [pair(kv_ref), (kc_ref, vc_ref)], finish))
    pl.when(jnp.logical_not(second))(lambda: attend(q_ref, [pair(kv_ref)], finish))


def far_kernel(q_ref, kv_ref, before_ref, out_ref):
    def finish(index, rows, *result):
        result = join(result, [before_ref[i, rows, :] for i in range(3)])
        for i in range(3):
            out_ref[i, rows, :] = result[i]

    attend(q_ref, [pair(kv_ref)], finish)


def last_kernel(q_ref, kv_ref, before_ref, out_ref, level_ref):
    def store(index, rows, mixture, total, peak):
        out_ref[rows, :] = mixture / total
        level_ref[level_rows(index), :] = level_of(peak, total)

    def finish(index, rows, *result):
        store(index, rows, *join(result, [before_ref[i, rows, :] for i in range(3)]))

    second = lax.axis_index("stretch") % 2 == 1

    @pl.when(second)
    def _():
        attend(q_ref, [pair(kv_ref)], finish)

    @pl.when(jnp.logical_not(second))
    def _():
        for index in range(q_ref.shape[0] // ROWS):
            rows = slice(index * ROWS, index * ROWS + ROWS)
            store(index, rows, *[before_ref[i, rows, :] for i in range(3)])


def even_chip():
    return lax.axis_index("stretch") < 2


def level_rows(index):
    return pl.ds(index * 8 if isinstance(index, int) else pl.multiple_of(index * 8, 8), 8)


def level_of(peak, total):
    level = (peak + jnp.log2(total)).T[:1, :]
    groups = [level[:, at : at + DH] for at in range(0, ROWS, DH)]
    return jnp.concatenate((groups * 8)[:8], axis=0)


def columns(*groups):
    lines = [
        jnp.concatenate([group[at : at + 1, :] for at in range(ROWS // DH)], axis=1)
        for group in groups
    ]
    lines += [lines[0]] * (8 - len(lines))
    table = jnp.concatenate(lines, axis=0).T
    return [table[:, at : at + 1] for at in range(len(groups))]


def message_rows(span):
    return span + 3 * level_count(span)


def level_count(span):
    return -(-span // ROWS * 8 // 16) * 16


def pack_level(ref, levels):
    count = levels.shape[0]
    rest = levels[...]
    for part in range(3):
        piece = rest.astype(BF16)
        rest = rest - piece.astype(F32)
        start = ref.shape[0] - (3 - part) * count
        ref[start : start + count, :] = piece


def unpack_level(ref, levels):
    count = levels.shape[0]
    parts = [
        ref[ref.shape[0] - (3 - part) * count : ref.shape[0] - (2 - part) * count, :].astype(F32)
        for part in range(3)
    ]
    levels[...] = parts[0] + parts[1] + parts[2]


def chip_near_kernel(q_ref, kv_ref, kc_ref, vc_ref, out_ref):
    def finish(index, rows, *result):
        for i in range(3):
            out_ref[i, rows, :] = result[i]

    @pl.when(even_chip())
    def _():
        attend(q_ref, [pair(kv_ref), (kc_ref, vc_ref)], finish)


def chip_far_kernel(block, q_ref, kv_ref, kvc_ref, near_ref, out_ref, levels):
    def finish(index, rows, *result):
        mixture, total, peak = join(result, [near_ref[i, rows, :] for i in range(3)])
        out_ref[:ROWS, :] = (mixture / total).astype(BF16)
        levels[level_rows(0), :] = level_of(peak, total)

    @pl.when(even_chip())
    def _():
        levels[...] = jnp.zeros_like(levels)
        attend(q_ref, [pair(kv_ref), pair(kvc_ref)], finish, block, 1)
        pack_level(out_ref, levels)


def merge_kernel(levels_ref, gate_ref, own_ref, level_ref, *refs):
    *chip_refs, out_ref, chip_levels = refs
    stretch = lax.axis_index("stretch")
    seq = lax.axis_index("seq")
    odd = stretch >= 2
    head = 16 * (seq // 32) + seq % 16
    lanes = pl.ds(pl.multiple_of(head * DH, DH), DH)
    noise = levels_ref[stretch]
    tile = gate_ref[pl.ds(pl.multiple_of(noise // 8 * 8, 8), 8), lanes]
    mine = lax.broadcasted_iota(jnp.int32, tile.shape, 0) == noise % 8
    gate = jnp.sum(jnp.where(mine, tile, 0.0), axis=0, keepdims=True)
    for index, chip_ref in enumerate(chip_refs):
        unpack_level(chip_ref, chip_levels)
        rows = slice(index * ROWS, index * ROWS + ROWS)
        level = level_ref[level_rows(index), :]
        chip_level = jnp.where(odd, chip_levels[level_rows(0), :], -jnp.inf)
        top = jnp.maximum(level, chip_level)
        left, right = jnp.exp2(level - top), jnp.exp2(chip_level - top)
        left, right = columns(left / (left + right), right / (left + right))
        other = jnp.where(odd, chip_ref[:ROWS, :].astype(F32), 0.0)
        attended = (own_ref[rows, :] * left + other * right).astype(BF16).astype(F32)
        out_ref[rows, :] = (gate * attended).astype(BF16)


HELD = pl.BlockSpec(memory_space=pltpu.VMEM)


def call(kernel, name, ins, in_specs, out_shape, out_spec, scratch, aliases=()):
    return pl.pallas_call(
        kernel,
        in_specs=in_specs,
        out_specs=out_spec,
        out_shape=out_shape,
        scratch_shapes=scratch,
        input_output_aliases=dict(aliases),
        compiler_params=pltpu.CompilerParams(vmem_limit_bytes=VMEM),
        cost_estimate=pl.CostEstimate(flops=DH, bytes_accessed=DH, transcendentals=0),
        name=name,
    )(*ins)


def local(queries, keys, values, levels, gate_table):
    tokens = queries.shape[1]
    half = tokens // 2
    span = 64 * half
    qkv = jnp.concatenate([queries, keys, values])
    qkv = qkv.reshape(3, 2, half, 2, 16, DH).transpose(3, 1, 4, 0, 2, 5).reshape(64, 3, half, DH)
    qkv = lax.all_to_all(qkv, "seq", 0, 0, tiled=True)
    qkv = qkv.transpose(1, 0, 2, 3).reshape(3, span, DH)
    q, kv = qkv[0], qkv[1:]

    core = exchange(1, 0)
    kv_x = send(kv, exchange(0, 16))
    kv_core = [send(kv[0], core), send(kv[1], core)]
    q_z = send(jnp.concatenate([q, kv[0, :64]]), exchange(2, 0, lambda stretch: stretch >= 2))
    state = jax.ShapeDtypeStruct((3, span, DH), F32)
    message = jax.ShapeDtypeStruct((message_rows(ROWS), DH), BF16)
    level_scratch = pltpu.VMEM((level_count(ROWS), DH), F32)
    own_shape = [
        jax.ShapeDtypeStruct((span, DH), F32), jax.ShapeDtypeStruct((level_count(span), DH), F32)
    ]
    near = call(near_kernel, "near", [q, kv, *kv_core], [HELD] * 4, state, HELD, [])
    q_z, near = lax.optimization_barrier((q_z, near))
    chip_near = call(
        chip_near_kernel, "chip_near", [q_z, kv, *kv_core], [HELD] * 4, state, HELD, []
    )
    kv_x, near, chip_near = lax.optimization_barrier((kv_x, near, chip_near))
    kv_x_core = send(kv_x, core)
    far = call(far_kernel, "far", [q, kv_x, near], [HELD] * 3, state, HELD, [], {2: 0})
    kv_x_core, far, chip_near = lax.optimization_barrier((kv_x_core, far, chip_near))

    def lend(block, before):
        chip = call(
            partial(chip_far_kernel, block), f"chip_far{block}", [q_z, kv_x, kv_x_core, before],
            [HELD] * 4, message, HELD, [level_scratch],
        )
        return chip, send(chip, exchange(2, 0, lambda stretch: stretch < 2))

    chip, first_in = lend(0, chip_near)
    chip, chip_near = lax.optimization_barrier((chip, chip_near))
    chip, second_in = lend(1, chip_near)
    first_in, chip, far = lax.optimization_barrier((first_in, chip, far))
    own = call(
        last_kernel, "last", [q, kv_x_core, far], [HELD] * 3, own_shape, [HELD] * 2, []
    )
    mixture = call(
        merge_kernel, "merge", [levels, gate_table, *own, first_in, second_in],
        [pl.BlockSpec(memory_space=pltpu.SMEM)] + [HELD] * 5,
        jax.ShapeDtypeStruct((span, DH), BF16), HELD, [level_scratch],
    )
    result = lax.all_to_all(mixture.reshape(64, half, DH), "seq", 0, 0, tiled=True)
    result = result.reshape(2, 2, 16, half, DH).transpose(1, 3, 0, 2, 4)
    return result.reshape(1, tokens, H * DH)


def solution(mesh):
    placed = (
        P("stretch", "seq", None),
        P("stretch", "seq", None),
        P("stretch", "seq", None),
        P(),
        P(),
    )
    return jax.shard_map(
        local, mesh=mesh, in_specs=placed, out_specs=P("stretch", "seq", None), check_vma=False
    )
```

```python
from functools import partial
import math

import jax
import jax.numpy as jnp
from jax import lax
from jax.experimental import pallas as pl
from jax.experimental.pallas import tpu as pltpu
from jax.sharding import PartitionSpec as P

H = 32
DH = 128
AXES = ("stretch", "seq")
SCALE = math.log2(math.e) / math.sqrt(DH)
ROWS = 768
KEYS = 512
VMEM = 24 * 2**20
F32 = jnp.float32
BF16 = jnp.bfloat16


def exchange(flip_stretch, flip_seq, keep=lambda stretch: True):
    return [
        (c * 64 + s, (c ^ flip_stretch) * 64 + (s ^ flip_seq))
        for c in range(4)
        for s in range(64)
        if keep(c)
    ]


def send(array, pairs):
    return lax.ppermute(array, AXES, pairs)


def score(q, key):
    return (
        lax.dot_general(q, key, (((1,), (1,)), ((), ())), preferred_element_type=F32) * SCALE
    )


def attend(q_ref, blocks, finish, first=0, count=None):
    work = [
        (key_ref, value_ref, at)
        for key_ref, value_ref in blocks
        for at in range(0, key_ref.shape[0], KEYS)
    ]

    def step(index, carry):
        rows = pl.ds(pl.multiple_of(index * ROWS, ROWS), ROWS)
        q = q_ref[rows, :]

        def scores_of(number):
            key_ref, _, at = work[number]
            return score(q, key_ref[at : at + KEYS, :])

        coming = scores_of(0)
        mixture = peak = None
        for number, (_, value_ref, at) in enumerate(work):
            scores = coming
            if number + 1 < len(work):
                coming = scores_of(number + 1)
            block_peak = jnp.max(scores, axis=1, keepdims=True)
            new_peak = block_peak if peak is None else jnp.maximum(peak, block_peak)
            weights = jnp.exp2(scores - new_peak).astype(BF16)
            value = value_ref[at : at + KEYS, :]
            value = jnp.concatenate([value, jnp.ones_like(value)], axis=1)
            part = jnp.dot(weights, value, preferred_element_type=F32)
            if peak is not None:
                part = mixture * jnp.exp2(peak - new_peak) + part
            mixture, peak = part, new_peak
        wide = jnp.broadcast_to(peak, (ROWS, DH))
        finish(index, rows, mixture[:, :DH], mixture[:, DH:], wide)
        return carry

    count = q_ref.shape[0] // ROWS if count is None else count
    lax.fori_loop(first, first + count, step, None)


def pair(ref):
    return ref.at[0], ref.at[1]


def join(first, second):
    peak = jnp.maximum(first[2], second[2])
    left, right = jnp.exp2(first[2] - peak), jnp.exp2(second[2] - peak)
    return (
        first[0] * left + second[0] * right,
        first[1] * left + second[1] * right,
        peak,
    )


def by_core(q_ref, blocks, core_block, finish):
    second = lax.axis_index("stretch") % 2 == 1
    pl.when(second)(lambda: attend(q_ref, [*blocks, core_block], finish))
    pl.when(jnp.logical_not(second))(lambda: attend(q_ref, blocks, finish))


def near_kernel(q_ref, kv_ref, kc_ref, vc_ref, out_ref):
    def finish(index, rows, *result):
        for i in range(3):
            out_ref[i, rows, :] = result[i]

    second = lax.axis_index("stretch") % 2 == 1
    pl.when(second)(lambda: attend(q_ref, [pair(kv_ref), (kc_ref, vc_ref)], finish))
    pl.when(jnp.logical_not(second))(lambda: attend(q_ref, [pair(kv_ref)], finish))


def add_block(q_ref, blocks, state_in, state_out):
    def finish(index, rows, *result):
        result = join(result, [state_in[i, rows, :] for i in range(3)])
        for i in range(3):
            state_out[i, rows, :] = result[i]

    attend(q_ref, blocks, finish)


def far_kernel(q_ref, q_z_ref, kv_ref, near_in, chip_in, near_out, chip_out):
    pl.when(even_chip())(lambda: add_block(q_z_ref, [pair(kv_ref)], chip_in, chip_out))
    pl.when(jnp.logical_not(even_chip()))(
        lambda: add_block(q_ref, [pair(kv_ref)], near_in, near_out)
    )


def last_kernel(q_ref, kv_ref, kvc_ref, before_ref, out_ref, level_ref):
    def store(index, rows, mixture, total, peak):
        out_ref[rows, :] = mixture / total
        level_ref[level_rows(index), :] = level_of(peak, total)

    def finish(index, rows, *result):
        store(index, rows, *join(result, [before_ref[i, rows, :] for i in range(3)]))

    second = lax.axis_index("stretch") % 2 == 1
    even = even_chip()
    odd = jnp.logical_not(even)
    first = jnp.logical_not(second)

    pl.when(even & second)(lambda: attend(q_ref, [pair(kv_ref), pair(kvc_ref)], finish))
    pl.when(even & first)(lambda: attend(q_ref, [pair(kv_ref)], finish))
    pl.when(odd & second)(lambda: attend(q_ref, [pair(kvc_ref)], finish))

    @pl.when(odd & first)
    def _():
        for index in range(q_ref.shape[0] // ROWS):
            rows = slice(index * ROWS, index * ROWS + ROWS)
            store(index, rows, *[before_ref[i, rows, :] for i in range(3)])


def even_chip():
    return lax.axis_index("stretch") < 2


def level_rows(index):
    return pl.ds(index * 8 if isinstance(index, int) else pl.multiple_of(index * 8, 8), 8)


def level_of(peak, total):
    level = (peak + jnp.log2(total)).T[:1, :]
    groups = [level[:, at : at + DH] for at in range(0, ROWS, DH)]
    return jnp.concatenate((groups * 8)[:8], axis=0)


def columns(*groups):
    lines = [
        jnp.concatenate([group[at : at + 1, :] for at in range(ROWS // DH)], axis=1)
        for group in groups
    ]
    lines += [lines[0]] * (8 - len(lines))
    table = jnp.concatenate(lines, axis=0).T
    return [table[:, at : at + 1] for at in range(len(groups))]


def message_rows(span):
    return span + 3 * level_count(span)


def level_count(span):
    return -(-span // ROWS * 8 // 16) * 16


def pack_level(ref, levels):
    count = levels.shape[0]
    rest = levels[...]
    for part in range(3):
        piece = rest.astype(BF16)
        rest = rest - piece.astype(F32)
        start = ref.shape[0] - (3 - part) * count
        ref[start : start + count, :] = piece


def unpack_level(ref, levels):
    count = levels.shape[0]
    parts = [
        ref[ref.shape[0] - (3 - part) * count : ref.shape[0] - (2 - part) * count, :].astype(F32)
        for part in range(3)
    ]
    levels[...] = parts[0] + parts[1] + parts[2]


def chip_near_kernel(q_ref, kv_ref, kc_ref, vc_ref, out_ref):
    def finish(index, rows, *result):
        for i in range(3):
            out_ref[i, rows, :] = result[i]

    @pl.when(even_chip())
    def _():
        attend(q_ref, [pair(kv_ref), (kc_ref, vc_ref)], finish)


def chip_far_kernel(block, q_ref, kvc_ref, near_ref, out_ref, levels):
    def finish(index, rows, *result):
        mixture, total, peak = join(result, [near_ref[i, rows, :] for i in range(3)])
        out_ref[:ROWS, :] = (mixture / total).astype(BF16)
        levels[level_rows(0), :] = level_of(peak, total)

    @pl.when(even_chip())
    def _():
        levels[...] = jnp.zeros_like(levels)
        attend(q_ref, [pair(kvc_ref)], finish, block, 1)
        pack_level(out_ref, levels)


def merge_kernel(levels_ref, gate_ref, own_ref, level_ref, *refs):
    *chip_refs, out_ref, chip_levels = refs
    stretch = lax.axis_index("stretch")
    seq = lax.axis_index("seq")
    odd = stretch >= 2
    head = 16 * (seq // 32) + seq % 16
    lanes = pl.ds(pl.multiple_of(head * DH, DH), DH)
    noise = levels_ref[stretch]
    tile = gate_ref[pl.ds(pl.multiple_of(noise // 8 * 8, 8), 8), lanes]
    mine = lax.broadcasted_iota(jnp.int32, tile.shape, 0) == noise % 8
    gate = jnp.sum(jnp.where(mine, tile, 0.0), axis=0, keepdims=True)
    for index, chip_ref in enumerate(chip_refs):
        unpack_level(chip_ref, chip_levels)
        rows = slice(index * ROWS, index * ROWS + ROWS)
        level = level_ref[level_rows(index), :]
        chip_level = jnp.where(odd, chip_levels[level_rows(0), :], -jnp.inf)
        top = jnp.maximum(level, chip_level)
        left, right = jnp.exp2(level - top), jnp.exp2(chip_level - top)
        left, right = columns(left / (left + right), right / (left + right))
        other = jnp.where(odd, chip_ref[:ROWS, :].astype(F32), 0.0)
        attended = (own_ref[rows, :] * left + other * right).astype(BF16).astype(F32)
        out_ref[rows, :] = (gate * attended).astype(BF16)


HELD = pl.BlockSpec(memory_space=pltpu.VMEM)


def call(kernel, name, ins, in_specs, out_shape, out_spec, scratch, aliases=()):
    return pl.pallas_call(
        kernel,
        in_specs=in_specs,
        out_specs=out_spec,
        out_shape=out_shape,
        scratch_shapes=scratch,
        input_output_aliases=dict(aliases),
        compiler_params=pltpu.CompilerParams(vmem_limit_bytes=VMEM),
        cost_estimate=pl.CostEstimate(flops=DH, bytes_accessed=DH, transcendentals=0),
        name=name,
    )(*ins)


def local(queries, keys, values, levels, gate_table):
    tokens = queries.shape[1]
    half = tokens // 2
    span = 64 * half
    qkv = jnp.concatenate([queries, keys, values])
    qkv = qkv.reshape(3, 2, half, 2, 16, DH).transpose(3, 1, 4, 0, 2, 5).reshape(64, 3, half, DH)
    qkv = lax.all_to_all(qkv, "seq", 0, 0, tiled=True)
    qkv = qkv.transpose(1, 0, 2, 3).reshape(3, span, DH)
    q, kv = qkv[0], qkv[1:]

    core = exchange(1, 0)
    kv_x = send(kv, exchange(0, 16))
    kv_core = [send(kv[0], core), send(kv[1], core)]
    q_z = send(jnp.concatenate([q, kv[0, :64]]), exchange(2, 0, lambda stretch: stretch >= 2))
    state = jax.ShapeDtypeStruct((3, span, DH), F32)
    message = jax.ShapeDtypeStruct((message_rows(ROWS), DH), BF16)
    level_scratch = pltpu.VMEM((level_count(ROWS), DH), F32)
    own_shape = [
        jax.ShapeDtypeStruct((span, DH), F32), jax.ShapeDtypeStruct((level_count(span), DH), F32)
    ]
    near = call(near_kernel, "near", [q, kv, *kv_core], [HELD] * 4, state, HELD, [])
    q_z, near = lax.optimization_barrier((q_z, near))
    chip_near = call(
        chip_near_kernel, "chip_near", [q_z, kv, *kv_core], [HELD] * 4, state, HELD, []
    )
    kv_x, near, chip_near = lax.optimization_barrier((kv_x, near, chip_near))
    kv_x_core = send(kv_x, core)
    far, chip_near = call(
        far_kernel, "far", [q, q_z, kv_x, near, chip_near], [HELD] * 5, [state] * 2, [HELD] * 2, [],
        {3: 0, 4: 1},
    )
    kv_x_core, far, chip_near = lax.optimization_barrier((kv_x_core, far, chip_near))

    def lend(block, before):
        chip = call(
            partial(chip_far_kernel, block), f"chip_far{block}", [q_z, kv_x_core, before],
            [HELD] * 3, message, HELD, [level_scratch],
        )
        return chip, send(chip, exchange(2, 0, lambda stretch: stretch < 2))

    chip, first_in = lend(0, chip_near)
    chip, chip_near = lax.optimization_barrier((chip, chip_near))
    chip, second_in = lend(1, chip_near)
    first_in, chip, far = lax.optimization_barrier((first_in, chip, far))
    own = call(
        last_kernel, "last", [q, kv_x, kv_x_core, far], [HELD] * 4, own_shape, [HELD] * 2, []
    )
    mixture = call(
        merge_kernel, "merge", [levels, gate_table, *own, first_in, second_in],
        [pl.BlockSpec(memory_space=pltpu.SMEM)] + [HELD] * 5,
        jax.ShapeDtypeStruct((span, DH), BF16), HELD, [level_scratch],
    )
    result = lax.all_to_all(mixture.reshape(64, half, DH), "seq", 0, 0, tiled=True)
    result = result.reshape(2, 2, 16, half, DH).transpose(1, 3, 0, 2, 4)
    return result.reshape(1, tokens, H * DH)


def solution(mesh):
    placed = (
        P("stretch", "seq", None),
        P("stretch", "seq", None),
        P("stretch", "seq", None),
        P(),
        P(),
    )
    return jax.shard_map(
        local, mesh=mesh, in_specs=placed, out_specs=P("stretch", "seq", None), check_vma=False
    )
```

```python
from functools import partial
import math

import jax
import jax.numpy as jnp
from jax import lax
from jax.experimental import pallas as pl
from jax.experimental.pallas import tpu as pltpu
from jax.sharding import PartitionSpec as P

H = 32
DH = 128
AXES = ("stretch", "seq")
SCALE = math.log2(math.e) / math.sqrt(DH)
ROWS = 768
KEYS = 512
VMEM = 24 * 2**20
F32 = jnp.float32
BF16 = jnp.bfloat16


def exchange(flip_stretch, flip_seq, keep=lambda stretch: True):
    return [
        (c * 64 + s, (c ^ flip_stretch) * 64 + (s ^ flip_seq))
        for c in range(4)
        for s in range(64)
        if keep(c)
    ]


def send(array, pairs):
    return lax.ppermute(array, AXES, pairs)


def score(q, key):
    return (
        lax.dot_general(q, key, (((1,), (1,)), ((), ())), preferred_element_type=F32) * SCALE
    )


def attend(q_ref, blocks, finish, first=0, count=None):
    work = [
        (key_ref, value_ref, at)
        for key_ref, value_ref in blocks
        for at in range(0, key_ref.shape[0], KEYS)
    ]

    def step(index, carry):
        rows = pl.ds(pl.multiple_of(index * ROWS, ROWS), ROWS)
        q = q_ref[rows, :]

        def scores_of(number):
            key_ref, _, at = work[number]
            return score(q, key_ref[at : at + KEYS, :])

        coming = scores_of(0)
        mixture = peak = None
        for number, (_, value_ref, at) in enumerate(work):
            scores = coming
            if number + 1 < len(work):
                coming = scores_of(number + 1)
            block_peak = jnp.max(scores, axis=1, keepdims=True)
            new_peak = block_peak if peak is None else jnp.maximum(peak, block_peak)
            weights = jnp.exp2(scores - new_peak).astype(BF16)
            value = value_ref[at : at + KEYS, :]
            value = jnp.concatenate([value, jnp.ones_like(value)], axis=1)
            part = jnp.dot(weights, value, preferred_element_type=F32)
            if peak is not None:
                part = mixture * jnp.exp2(peak - new_peak) + part
            mixture, peak = part, new_peak
        wide = jnp.broadcast_to(peak, (ROWS, DH))
        finish(index, rows, mixture[:, :DH], mixture[:, DH:], wide)
        return carry

    count = q_ref.shape[0] // ROWS if count is None else count
    lax.fori_loop(first, first + count, step, None)


def pair(ref):
    return ref.at[0], ref.at[1]


def join(first, second):
    peak = jnp.maximum(first[2], second[2])
    left, right = jnp.exp2(first[2] - peak), jnp.exp2(second[2] - peak)
    return (
        first[0] * left + second[0] * right,
        first[1] * left + second[1] * right,
        peak,
    )


def by_core(q_ref, blocks, core_block, finish):
    second = lax.axis_index("stretch") % 2 == 1
    pl.when(second)(lambda: attend(q_ref, [*blocks, core_block], finish))
    pl.when(jnp.logical_not(second))(lambda: attend(q_ref, blocks, finish))


def near_kernel(q_ref, kv_ref, kc_ref, vc_ref, out_ref):
    def finish(index, rows, *result):
        for i in range(3):
            out_ref[i, rows, :] = result[i]

    second = lax.axis_index("stretch") % 2 == 1
    pl.when(second)(lambda: attend(q_ref, [pair(kv_ref), (kc_ref, vc_ref)], finish))
    pl.when(jnp.logical_not(second))(lambda: attend(q_ref, [pair(kv_ref)], finish))


def far_kernel(q_ref, kv_ref, before_ref, out_ref):
    def finish(index, rows, *result):
        result = join(result, [before_ref[i, rows, :] for i in range(3)])
        for i in range(3):
            out_ref[i, rows, :] = result[i]

    attend(q_ref, [pair(kv_ref)], finish)


def last_kernel(q_ref, kv_ref, before_ref, out_ref, level_ref):
    def store(index, rows, mixture, total, peak):
        out_ref[rows, :] = mixture / total
        level_ref[level_rows(index), :] = level_of(peak, total)

    def finish(index, rows, *result):
        store(index, rows, *join(result, [before_ref[i, rows, :] for i in range(3)]))

    second = lax.axis_index("stretch") % 2 == 1

    @pl.when(second)
    def _():
        attend(q_ref, [pair(kv_ref)], finish)

    @pl.when(jnp.logical_not(second))
    def _():
        for index in range(q_ref.shape[0] // ROWS):
            rows = slice(index * ROWS, index * ROWS + ROWS)
            store(index, rows, *[before_ref[i, rows, :] for i in range(3)])


def even_chip():
    return lax.axis_index("stretch") < 2


def level_rows(index):
    return pl.ds(index * 8 if isinstance(index, int) else pl.multiple_of(index * 8, 8), 8)


def level_of(peak, total):
    level = (peak + jnp.log2(total)).T[:1, :]
    groups = [level[:, at : at + DH] for at in range(0, ROWS, DH)]
    return jnp.concatenate((groups * 8)[:8], axis=0)


def columns(*groups):
    lines = [
        jnp.concatenate([group[at : at + 1, :] for at in range(ROWS // DH)], axis=1)
        for group in groups
    ]
    lines += [lines[0]] * (8 - len(lines))
    table = jnp.concatenate(lines, axis=0).T
    return [table[:, at : at + 1] for at in range(len(groups))]


def message_rows(span):
    return span + 3 * level_count(span)


def level_count(span):
    return -(-span // ROWS * 8 // 16) * 16


def pack_level(ref, levels):
    count = levels.shape[0]
    rest = levels[...]
    for part in range(3):
        piece = rest.astype(BF16)
        rest = rest - piece.astype(F32)
        start = ref.shape[0] - (3 - part) * count
        ref[start : start + count, :] = piece


def unpack_level(ref, levels):
    count = levels.shape[0]
    parts = [
        ref[ref.shape[0] - (3 - part) * count : ref.shape[0] - (2 - part) * count, :].astype(F32)
        for part in range(3)
    ]
    levels[...] = parts[0] + parts[1] + parts[2]


def chip_near_kernel(q_ref, kv_ref, kc_ref, vc_ref, out_ref):
    def finish(index, rows, *result):
        for i in range(3):
            out_ref[i, rows, :] = result[i]

    @pl.when(even_chip())
    def _():
        attend(q_ref, [pair(kv_ref), (kc_ref, vc_ref)], finish)


def chip_far_kernel(block, q_ref, kv_ref, kvc_ref, near_ref, out_ref, levels):
    def finish(index, rows, *result):
        mixture, total, peak = join(result, [near_ref[i, rows, :] for i in range(3)])
        out_ref[:ROWS, :] = (mixture / total).astype(BF16)
        levels[level_rows(0), :] = level_of(peak, total)

    @pl.when(even_chip())
    def _():
        levels[...] = jnp.zeros_like(levels)
        attend(q_ref, [pair(kv_ref), pair(kvc_ref)], finish, block, 1)
        pack_level(out_ref, levels)


def merge_kernel(levels_ref, gate_ref, own_ref, level_ref, *refs):
    *chip_refs, out_ref, chip_levels = refs
    stretch = lax.axis_index("stretch")
    seq = lax.axis_index("seq")
    odd = stretch >= 2
    head = 16 * (seq // 32) + seq % 16
    lanes = pl.ds(pl.multiple_of(head * DH, DH), DH)
    noise = levels_ref[stretch]
    tile = gate_ref[pl.ds(pl.multiple_of(noise // 8 * 8, 8), 8), lanes]
    mine = lax.broadcasted_iota(jnp.int32, tile.shape, 0) == noise % 8
    gate = jnp.sum(jnp.where(mine, tile, 0.0), axis=0, keepdims=True)
    for index, chip_ref in enumerate(chip_refs):
        unpack_level(chip_ref, chip_levels)
        rows = slice(index * ROWS, index * ROWS + ROWS)
        level = level_ref[level_rows(index), :]
        chip_level = jnp.where(odd, chip_levels[level_rows(0), :], -jnp.inf)
        top = jnp.maximum(level, chip_level)
        left, right = jnp.exp2(level - top), jnp.exp2(chip_level - top)
        left, right = columns(left / (left + right), right / (left + right))
        other = jnp.where(odd, chip_ref[:ROWS, :].astype(F32), 0.0)
        attended = (own_ref[rows, :] * left + other * right).astype(BF16).astype(F32)
        out_ref[rows, :] = (gate * attended).astype(BF16)


HELD = pl.BlockSpec(memory_space=pltpu.VMEM)


def call(kernel, name, ins, in_specs, out_shape, out_spec, scratch, aliases=()):
    return pl.pallas_call(
        kernel,
        in_specs=in_specs,
        out_specs=out_spec,
        out_shape=out_shape,
        scratch_shapes=scratch,
        input_output_aliases=dict(aliases),
        compiler_params=pltpu.CompilerParams(vmem_limit_bytes=VMEM),
        cost_estimate=pl.CostEstimate(flops=DH, bytes_accessed=DH, transcendentals=0),
        name=name,
    )(*ins)


def local(queries, keys, values, levels, gate_table):
    tokens = queries.shape[1]
    half = tokens // 2
    span = 64 * half
    qkv = jnp.concatenate([queries, keys, values])
    qkv = qkv.reshape(3, 2, half, 2, 16, DH).transpose(3, 1, 4, 0, 2, 5).reshape(64, 3, half, DH)
    qkv = lax.all_to_all(qkv, "seq", 0, 0, tiled=True)
    qkv = qkv.transpose(1, 0, 2, 3).reshape(3, span, DH)
    q, kv = qkv[0], qkv[1:]

    core = exchange(1, 0)
    kv_x = send(kv, exchange(0, 16))
    kv_core = [send(kv[0], core), send(kv[1], core)]
    q_z = send(jnp.concatenate([q, kv[0, :64]]), exchange(2, 0, lambda stretch: stretch >= 2))
    state = jax.ShapeDtypeStruct((3, span, DH), F32)
    message = jax.ShapeDtypeStruct((message_rows(ROWS), DH), BF16)
    level_scratch = pltpu.VMEM((level_count(ROWS), DH), F32)
    own_shape = [
        jax.ShapeDtypeStruct((span, DH), F32), jax.ShapeDtypeStruct((level_count(span), DH), F32)
    ]
    near = call(near_kernel, "near", [q, kv, *kv_core], [HELD] * 4, state, HELD, [])
    q_z, near = lax.optimization_barrier((q_z, near))
    chip_near = call(
        chip_near_kernel, "chip_near", [q_z, kv, *kv_core], [HELD] * 4, state, HELD, []
    )
    kv_x, near, chip_near = lax.optimization_barrier((kv_x, near, chip_near))
    kv_x_core = send(kv_x, core)
    far = call(far_kernel, "far", [q, kv_x, near], [HELD] * 3, state, HELD, [], {2: 0})
    kv_x_core, far, chip_near = lax.optimization_barrier((kv_x_core, far, chip_near))

    def lend(block, before):
        chip = call(
            partial(chip_far_kernel, block), f"chip_far{block}", [q_z, kv_x, kv_x_core, before],
            [HELD] * 4, message, HELD, [level_scratch],
        )
        return chip, send(chip, exchange(2, 0, lambda stretch: stretch < 2))

    chip, first_in = lend(0, chip_near)
    chip, chip_near = lax.optimization_barrier((chip, chip_near))
    chip, second_in = lend(1, chip_near)
    chip, far = lax.optimization_barrier((chip, far))
    own = call(
        last_kernel, "last", [q, kv_x_core, far], [HELD] * 3, own_shape, [HELD] * 2, []
    )
    mixture = call(
        merge_kernel, "merge", [levels, gate_table, *own, first_in, second_in],
        [pl.BlockSpec(memory_space=pltpu.SMEM)] + [HELD] * 5,
        jax.ShapeDtypeStruct((span, DH), BF16), HELD, [level_scratch],
    )
    result = lax.all_to_all(mixture.reshape(64, half, DH), "seq", 0, 0, tiled=True)
    result = result.reshape(2, 2, 16, half, DH).transpose(1, 3, 0, 2, 4)
    return result.reshape(1, tokens, H * DH)


def solution(mesh):
    placed = (
        P("stretch", "seq", None),
        P("stretch", "seq", None),
        P("stretch", "seq", None),
        P(),
        P(),
    )
    return jax.shard_map(
        local, mesh=mesh, in_specs=placed, out_specs=P("stretch", "seq", None), check_vma=False
    )
```
